32 devices in a mesh: inner: 4 (over x, core), outer: 8 (over z, y).
Axes of the slice: x: 2, y: 2, z: 4, core: 2. Of those that a mesh axis runs over, the one named last changes fastest.
Arguments:
- out_grad: bfloat16 [4096, 2048], P(('inner', 'outer')), may hold values from -6 to 6
- expert_ids: int32 [4096, 8], P(('inner', 'outer')), may hold values from 0 to 31, all different within a row; in each aligned block of 128 rows (0 to 127, 128 to 255, ...) at most 40 rows name the same one
- gates: float32 [4096, 8], P(('inner', 'outer')), may hold values from 0.05 to 0.5
- expert_input: bfloat16 [32, 32, 40, 2048], P(None, ('inner', 'outer')), may hold values from -6 to 6
- gate_up_weight: bfloat16 [32, 2048, 1536], P(('inner', 'outer')), may hold values from -0.125 to 0.125
- down_weight: bfloat16 [32, 768, 2048], P(('inner', 'outer')), may hold values from -0.21875 to 0.21875
Outputs:
- token_grad: bfloat16 [4096, 2048], P(('inner', 'outer'))
- down_grad: bfloat16 [32, 768, 2048], P(('inner', 'outer'))
The draws below stay inside these ranges and needn't reach their ends.
Inputs may be any that keep to these rules, and one draw needn't show every extreme that they name: `expert_ids`: within each aligned block of 128 tokens (the tokens of one device) the 8 experts of a token differ, no expert is named by more than 40 pairs, a bound that some block reaches; every expert is named somewhere.
All inputs are finite; a program needn't handle non-finite values.
Results may differ from the reference program's by a relative error of at most 0.0064.
Values may be sent and summed in bfloat16 or wider, within the bound.
A program may use at most 128 MiB of HBM per device.

```python
import math
import jax
import jax.numpy as jnp
import numpy as np
from jax import lax

D = 2048
H = 768
TOP = 8
TOK_DEV = 128
EXPERTS = 32
TOKENS = 4096
CPS = 40
DEVICES = 32


def level_of(rng, extent, pieces, smallest, top_value):
    def one(axis_at, shards_of):
        steps = jax.random.uniform(jax.random.fold_in(jax.random.fold_in(rng, 6), axis_at), (shards_of,), jnp.float32, smallest / len(pieces), top_value / len(pieces))
        return jnp.repeat(jnp.exp(steps), extent[axis_at] // shards_of).reshape((-1,) + (1,) * (len(extent) - axis_at - 1))

    level = one(*pieces[0])
    for cut in pieces[1:]:
        level = level * one(*cut)
    return level


def assign_block(rng, own, number, rows, count, top, bound, lean):
    ranking = jax.random.permutation(rng, count)
    crowded, common = portions_of(count, rows * top, bound, lean, True), portions_of(count, rows * top, bound, lean, False)
    places = jnp.arange(count)

    def named(lengths, rotation):
        used = int((lengths > 0).sum())
        fixed = max(1, used // 4)
        moved = fixed + (places - fixed + rotation * (used - fixed)) % max(1, count - fixed)
        return jnp.zeros((count,), jnp.int32).at[ranking[jnp.where(places < fixed, places, moved)]].set(jnp.asarray(lengths, jnp.int32))

    lengths = jnp.where(number % 4 == 0, named(crowded, number // 4), named(common, number - number // 4 - 1))
    mixed = jax.random.permutation(jax.random.fold_in(own, 3), count)
    donor, taker = mixed[0:count // 2 * 2:2], mixed[1:count // 2 * 2:2]
    slack = jnp.minimum(lengths[donor] - 1, bound - lengths[taker]) // 2
    slack = jnp.where((donor == ranking[0]) | (taker == ranking[0]) | (lengths[taker] == 0), 0, jnp.maximum(slack, 0))
    moved = jax.random.randint(jax.random.fold_in(own, 4), (count // 2,), 0, 1 << 20) % (slack + 1)
    lengths = lengths.at[donor].add(-moved).at[taker].add(moved)
    labels = jnp.searchsorted(jnp.cumsum(lengths), jnp.arange(rows * top), side="right").astype(jnp.int32)
    grid = labels.reshape(top, rows).T
    grid = grid[jax.random.permutation(jax.random.fold_in(own, 1), rows)]
    rotation = jax.random.randint(jax.random.fold_in(own, 2), (rows, 1), 0, top)
    return jnp.take_along_axis(grid, (jnp.arange(top)[None, :] + rotation) % top, axis=1)


def portions_of(count, total, bound, skew, full):
    loads = [(1 << 20) // math.isqrt(standing ** skew) + 1 for standing in range(1, count + 1)]
    largest = bound if full else min(bound, max(-(-total // count), total * loads[0] // sum(loads)))
    least = 1 if total - largest >= count - 1 else 0
    counts, rest = [largest] + [least] * (count - 1), total - largest - least * (count - 1)
    while rest > 0:
        free = [i for i in range(1, count) if counts[i] < largest] or [i for i in range(1, count) if counts[i] < bound]
        mass, left = sum([loads[i] for i in free]), rest
        for i in free:
            addition = min(bound - counts[i], max(1, left * loads[i] // mass), rest)
            counts[i] = counts[i] + addition
            rest = rest - addition
    return np.array(counts)


def normal_values(stream_key, shape, spread, bound, cuts=(), held_as=jnp.bfloat16):
    drawn = spread * jax.random.normal(stream_key, shape, jnp.float32)
    if cuts:
        drawn = drawn * level_of(stream_key, shape, cuts, -0.22, 0.18)
    return jnp.clip(drawn, -bound, bound).astype(held_as)


def setup_inputs(seed: int = 0) -> dict:
    key_list = jax.random.split(jax.random.key(seed), 7)
    out_grad = normal_values(key_list[0], (TOKENS, D), 1.0, 6.0, ((0, 32),))
    expert_ids_keys = jax.random.split(jax.random.fold_in(key_list[1], 1), TOKENS // TOK_DEV)
    expert_ids_turns = jax.random.permutation(jax.random.fold_in(key_list[1], 3), TOKENS // TOK_DEV)
    expert_ids = jax.vmap(lambda own, number: assign_block(jax.random.fold_in(key_list[1], 2), own, number, TOK_DEV, EXPERTS, TOP, CPS, 2))(expert_ids_keys, expert_ids_turns).reshape((TOKENS, TOP))
    gates = jnp.clip(0.05 + 0.45 * jax.random.uniform(key_list[2], (TOKENS, TOP), jnp.float32) ** level_of(key_list[2], (TOKENS, TOP), ((0, 32),), -0.2, 0.2), 0.05, 0.5)
    expert_input = normal_values(key_list[3], (DEVICES, EXPERTS, CPS, D), 1.0, 6.0, ((1, 32),))
    gate_up_weight = normal_values(key_list[4], (EXPERTS, D, 2 * H), D ** -0.5, 0.125, ((0, 32),))
    down_weight = normal_values(key_list[5], (EXPERTS, H, D), H ** -0.5, 0.21875, ((0, 32),))
    return dict(out_grad=out_grad, expert_ids=expert_ids, gates=gates, expert_input=expert_input, gate_up_weight=gate_up_weight, down_weight=down_weight)


def slot_of(block_ids, count):
    flat_ids = block_ids.reshape(-1)
    onehot = (flat_ids[:, None] == jnp.arange(count, dtype=jnp.int32)[None, :]).astype(jnp.int32)
    ranks = jnp.cumsum(onehot, axis=0) - 1
    return jnp.sum(ranks * onehot, axis=1).astype(jnp.int32)


def expert_backward(inputs, rows, gate_up, down):
    hidden_width = down.shape[0]
    pre = jnp.dot(inputs, gate_up, preferred_element_type=jnp.float32)
    act_a = pre[:, :hidden_width]
    act_b = pre[:, hidden_width:]
    sigma = jax.nn.sigmoid(act_a)
    silu_a = act_a * sigma
    hidden = (silu_a * act_b).astype(jnp.bfloat16)
    grad_h = lax.dot_general(rows, down, (((1,), (1,)), ((), ())), preferred_element_type=jnp.float32)
    grad_a = grad_h * act_b * sigma * (1.0 + act_a * (1.0 - sigma))
    grad_b = grad_h * silu_a
    grad_gu = jnp.concatenate([grad_a, grad_b], axis=1).astype(jnp.bfloat16)
    slot_grad = lax.dot_general(grad_gu, gate_up, (((1,), (1,)), ((), ())), preferred_element_type=jnp.float32).astype(jnp.bfloat16)
    down_grad = lax.dot_general(hidden, rows, (((0,), (0,)), ((), ())), preferred_element_type=jnp.float32).astype(jnp.bfloat16)
    return slot_grad, down_grad


def reference(out_grad, expert_ids, gates, expert_input, gate_up_weight, down_weight):
    blocks_ids = expert_ids.reshape(DEVICES, TOK_DEV, TOP)
    blocks_gates = gates.reshape(DEVICES, TOK_DEV, TOP)
    blocks_grad = out_grad.reshape(DEVICES, TOK_DEV, D)

    def dispatch_block(items):
        block_ids, block_gates, block_grad = items
        dest = (block_ids.reshape(-1) * CPS + slot_of(block_ids, EXPERTS)).astype(jnp.int32)
        scaled = (block_gates[:, :, None] * block_grad[:, None, :].astype(jnp.float32)).astype(jnp.bfloat16)
        empty = jnp.zeros((EXPERTS * CPS, D), jnp.bfloat16)
        return empty.at[dest].set(scaled.reshape(TOK_DEV * TOP, D))

    dispatched = lax.map(dispatch_block, (blocks_ids, blocks_gates, blocks_grad))
    dispatched = dispatched.reshape(DEVICES, EXPERTS, CPS, D)

    def one_expert(index):
        inputs = lax.dynamic_index_in_dim(expert_input, index, 1, keepdims=False).reshape(DEVICES * CPS, D)
        rows = lax.dynamic_index_in_dim(dispatched, index, 1, keepdims=False).reshape(DEVICES * CPS, D)
        gate_up = lax.dynamic_index_in_dim(gate_up_weight, index, 0, keepdims=False)
        down = lax.dynamic_index_in_dim(down_weight, index, 0, keepdims=False)
        slot_grad, down_grad = expert_backward(inputs, rows, gate_up, down)
        return slot_grad.reshape(DEVICES, CPS, D), down_grad

    slot_grads, down_grad = lax.map(one_expert, jnp.arange(EXPERTS, dtype=jnp.int32))

    def combine_block(items):
        block_ids, source = items
        flat_ids = block_ids.reshape(-1)
        slots = slot_of(block_ids, EXPERTS)
        sources = jnp.zeros_like(flat_ids) + source
        picked = slot_grads[flat_ids, sources, slots].astype(jnp.float32)
        return jnp.sum(picked.reshape(TOK_DEV, TOP, D), axis=1).astype(jnp.bfloat16)

    token_grad = lax.map(combine_block, (blocks_ids, jnp.arange(DEVICES, dtype=jnp.int32)))
    return token_grad.reshape(TOKENS, D), down_grad
```

```python
import jax
import jax.numpy as jnp
from jax import lax
from jax.sharding import Mesh, PartitionSpec as P

PLANE = ("i", "n")


def routing_maps(ids, gates, count):
    tok = ids.shape[0]
    chosen = ids[:, :, None] == jnp.arange(count, dtype=jnp.int32)
    named = jnp.any(chosen, axis=1)
    before = jnp.arange(tok)[:, None] > jnp.arange(tok)[None, :]
    slot = jnp.dot(
        before.astype(jnp.bfloat16), named.astype(jnp.bfloat16), preferred_element_type=jnp.float32
    )
    slot = jnp.where(named, slot, -1.0)
    gate = jnp.sum(jnp.where(chosen, gates[:, :, None], 0.0), axis=1)
    return slot.T, gate.T


def per_device(out_grad, expert_ids, gates, expert_input, gate_up_weight, down_weight):
    inner, major, minor = lax.axis_size("i"), lax.axis_size("m"), lax.axis_size("n")
    plane = inner * minor
    tok = expert_ids.shape[0]
    sources, _, cps, width = expert_input.shape
    slot, gate = routing_maps(expert_ids, gates, sources)
    maps = jnp.stack([slot, gate]).reshape(2, inner, major, minor, tok).transpose(2, 0, 1, 3, 4)
    maps = lax.all_to_all(maps, "m", split_axis=0, concat_axis=0, tiled=True)
    slot, gate = maps[:, 0].reshape(major, plane, tok), maps[:, 1].reshape(major, plane, tok)
    blocks = lax.all_gather(out_grad, "m")
    pick = slot[:, :, None, :] == jnp.arange(cps, dtype=jnp.float32)[:, None]
    scale = jnp.sum(jnp.where(pick, gate[:, :, None, :], 0.0), axis=-1)
    pick = pick.astype(jnp.bfloat16)
    rows = jnp.einsum("mpct,mtd->pmcd", pick, blocks, preferred_element_type=jnp.float32)
    rows = (rows * scale.transpose(1, 0, 2)[..., None]).astype(jnp.bfloat16)
    rows = lax.all_to_all(rows, PLANE, split_axis=0, concat_axis=0, tiled=True)
    rows = rows.reshape(sources * cps, width)
    inputs = expert_input.reshape(inner, major, minor, cps, width).transpose(0, 2, 1, 3, 4)
    inputs = inputs.reshape(sources * cps, width)

    gate_up, down = gate_up_weight[0], down_weight[0]
    hidden_width = down.shape[0]
    pre = jnp.dot(inputs, gate_up, preferred_element_type=jnp.float32)
    act_a, act_b = pre[:, :hidden_width], pre[:, hidden_width:]
    sigma = jax.nn.sigmoid(act_a)
    silu_a = act_a * sigma
    hidden = (silu_a * act_b).astype(jnp.bfloat16)
    grad_h = lax.dot_general(
        rows, down, (((1,), (1,)), ((), ())), preferred_element_type=jnp.float32
    )
    grad_a = grad_h * act_b * sigma * (1.0 + act_a * (1.0 - sigma))
    grad_gu = jnp.concatenate([grad_a, grad_h * silu_a], axis=1).astype(jnp.bfloat16)
    slot_grad = lax.dot_general(
        grad_gu, gate_up, (((1,), (1,)), ((), ())), preferred_element_type=jnp.float32
    ).astype(jnp.bfloat16)
    down_grad = lax.dot_general(
        hidden, rows, (((0,), (0,)), ((), ())), preferred_element_type=jnp.float32
    ).astype(jnp.bfloat16)

    back = slot_grad.reshape(plane, major, cps, width)
    back = lax.all_to_all(back, PLANE, split_axis=0, concat_axis=0, tiled=True)
    part = jnp.einsum("mpct,pmcd->mtd", pick, back, preferred_element_type=jnp.float32)
    part = part.astype(jnp.bfloat16)
    part = lax.all_to_all(part, "m", split_axis=0, concat_axis=0, tiled=True)
    token_grad = jnp.sum(part.astype(jnp.float32), axis=0).astype(jnp.bfloat16)
    return token_grad, down_grad[None]


def solution(mesh):
    inner, outer = mesh.devices.shape
    major = 4
    fine = Mesh(mesh.devices.reshape(inner, major, outer // major), ("i", "m", "n"))
    every = ("i", "m", "n")
    placed = (
        P(every, None),
        P(every, None),
        P(every, None),
        P(None, every, None, None),
        P(every, None, None),
        P(every, None, None),
    )
    return jax.shard_map(
        per_device,
        mesh=fine,
        in_specs=placed,
        out_specs=(P(every, None), P(every, None, None)),
        check_vma=False,
    )
```

```python
import functools

import jax
import jax.numpy as jnp
from jax import lax
from jax.experimental import pallas as pl
from jax.experimental.pallas import tpu as pltpu
from jax.sharding import Mesh, PartitionSpec as P

PLANE = ("i", "n")
MESH = pl.DeviceIdType.MESH
F32, BF16 = jnp.float32, jnp.bfloat16
LANES = 512


def fused_kernel(
    cps, og_in, maps_in, x_in, wgu_in, wd_in, token_out, down_out,
    og, maps, pick, scale, send, rows, xs, back, pre, wgu, wd, dgu, hid, own, part, got,
    load_sem, copy_sem, zs_sem, zr_sem, ms_sem, mr_sem, ds_sem, dr_sem, cs_sem, cr_sem, ps_sem, pr_sem,
):
    i, m, n = lax.axis_index("i"), lax.axis_index("m"), lax.axis_index("n")
    x, c = i // 2, i % 2
    zh, zl = m // 2, m % 2
    mine = i * 2 + n
    tok, width = og_in.shape
    hidden_width = wd_in.shape[0]
    pair = 2 * cps
    total = 8 * pair
    early = cps // 16 * 16
    late = pair - early
    early_at = pl.multiple_of(zl * late, 16)
    late_at = pl.multiple_of((1 - zl) * early, 16)

    def z_peer(j):
        return 2 * ((zh + j // 2) % 2) + (zl + j % 2) % 2

    def plane_peer(k):
        ki, kc, kn = k // 4, k // 2 % 2, k % 2
        return 2 * ((x + ki) % 2) + (c + kc) % 2, (n + kn) % 2

    def block_rows(which):
        return pl.ds(pl.multiple_of(which * tok, tok), tok)

    loads = [
        pltpu.make_async_copy(og_in, og.at[0, block_rows(zl)], load_sem.at[0]),
        pltpu.make_async_copy(maps_in.at[m], maps.at[0, zl], load_sem.at[1]),
        pltpu.make_async_copy(wgu_in, wgu, load_sem.at[2]),
    ]
    for g in range(2):
        for a in range(4):
            loads.append(
                pltpu.make_async_copy(
                    x_in.at[a, pl.ds(2 * ((zh + g) % 2), 2)],
                    xs.at[g, pl.ds(2 * a, 2)],
                    load_sem.at[3 + 4 * g + a],
                )
            )
    loads.append(pltpu.make_async_copy(wd_in, wd, load_sem.at[11]))
    for load in loads:
        load.start()

    barrier = pltpu.get_barrier_semaphore()
    for j in range(1, 4):
        pl.semaphore_signal(barrier, inc=1, device_id=(i, z_peer(j), n), device_id_type=MESH)
    for k in range(1, 8):
        pi, pn = plane_peer(k)
        pl.semaphore_signal(barrier, inc=1, device_id=(pi, m, pn), device_id_type=MESH)
    pl.semaphore_wait(barrier, 10)

    map_copies, block_copies = [], []
    for j in range(1, 4):
        there = z_peer(j)
        map_copies.append(
            pltpu.make_async_remote_copy(
                src_ref=maps_in.at[there], dst_ref=maps.at[j // 2, zl],
                send_sem=ms_sem.at[j], recv_sem=mr_sem.at[j],
                device_id=(i, there, n), device_id_type=MESH,
            )
        )
        block_copies.append(
            pltpu.make_async_remote_copy(
                src_ref=og_in, dst_ref=og.at[j // 2, block_rows(zl)],
                send_sem=zs_sem.at[j], recv_sem=zr_sem.at[j],
                device_id=(i, there, n), device_id_type=MESH,
            )
        )
    for copy in map_copies + block_copies:
        copy.start()

    loads[1].wait()
    for copy in map_copies:
        copy.wait_recv()
    place = lax.broadcasted_iota(jnp.int32, (pair, 2 * tok), 0).astype(F32)
    for g in range(2):
        for p in range(8):
            slot = jnp.concatenate([maps[g, 0, p : p + 1, :], maps[g, 1, p : p + 1, :] + cps], axis=1)
            gate = jnp.concatenate([maps[g, 0, 8 + p : 9 + p, :], maps[g, 1, 8 + p : 9 + p, :]], axis=1)
            hit = place == slot
            pick[g, p] = jnp.where(hit, 1.0, 0.0).astype(BF16)
            factor = jnp.sum(jnp.where(hit, gate, 0.0), axis=1, keepdims=True)
            scale[g, p] = jnp.broadcast_to(factor, (pair, 128))

    def lanes(t, size=LANES):
        return pl.ds(pl.multiple_of(t * size, size), size)

    order = (5, 7, 4, 1, 6, 3, 2)
    sent = []

    def dispatch(g, chunk, start, size, whole):
        tokens = slice(None) if whole else block_rows(zl)
        depth = 2 * tok if whole else tok
        weights = pick[g, :, pl.ds(start, size), tokens].reshape(8 * size, depth)
        factor = scale[g, :, pl.ds(start, size), :].reshape(8 * size, 128)[:, :1]

        def tile(t, _):
            out = jnp.dot(weights, og[g, tokens, lanes(t)], preferred_element_type=F32) * factor
            send[g, :, pl.ds(start, size), lanes(t)] = out.astype(BF16).reshape(8, size, LANES)
            return 0

        lax.fori_loop(0, width // LANES, tile, 0)
        copies = []
        for k in order:
            pi, pn = plane_peer(k)
            copy = pltpu.make_async_remote_copy(
                src_ref=send.at[g, pi * 2 + pn, pl.ds(start, size)],
                dst_ref=rows.at[g, mine, pl.ds(start, size)],
                send_sem=ds_sem.at[g, chunk, k], recv_sem=dr_sem.at[g, chunk, k],
                device_id=(pi, m, pn), device_id_type=MESH,
            )
            copy.start()
            copies.append(copy)
        here = pltpu.make_async_copy(
            send.at[g, mine, pl.ds(start, size)], rows.at[g, mine, pl.ds(start, size)], copy_sem.at[g, chunk]
        )
        here.start()
        sent.extend(copies)
        return copies, here

    def forward(g):
        for a in range(4):
            loads[3 + 4 * g + a].wait()

        def tile(t, _):
            out = jnp.dot(
                xs[g].reshape(total, width), wgu[:, lanes(t)], preferred_element_type=F32
            ).reshape(4, 4, cps, LANES)
            for a in range(2):
                for b in range(2):
                    pre[g, :, b * 2 + a, :, lanes(t)] = out[:, a * 2 + b]
            return 0

        lax.fori_loop(0, 2 * hidden_width // LANES, tile, 0)

    def backward(g, arriving):
        for copies, here in arriving:
            for copy in copies:
                copy.wait_recv()
            here.wait()

        def first(t, _):
            size = 256
            at_b = pl.ds(pl.multiple_of(hidden_width + t * size, size), size)
            grad_h = lax.dot_general(
                rows[g].reshape(total, width), wd[lanes(t, size), :], (((1,), (1,)), ((), ())),
                preferred_element_type=F32,
            )
            act_a = pre[g, :, :, :, lanes(t, size)].reshape(total, size)
            act_b = pre[g, :, :, :, at_b].reshape(total, size)
            sigma = jax.nn.sigmoid(act_a)
            silu_a = act_a * sigma
            hid[g, :, lanes(t, size)] = (silu_a * act_b).astype(BF16)
            dgu[:, lanes(t, size)] = (
                grad_h * act_b * sigma * (1.0 + act_a * (1.0 - sigma))
            ).astype(BF16)
            dgu[:, at_b] = (grad_h * silu_a).astype(BF16)
            return 0

        lax.fori_loop(0, hidden_width // 256, first, 0)
        copies = []
        half = width // 2
        for h in range(2):
            def second(t, _):
                out = lax.dot_general(
                    dgu[...], wgu[lanes(t), :], (((1,), (1,)), ((), ())), preferred_element_type=F32
                )
                xs[g, :, :, lanes(t)] = out.astype(BF16).reshape(8, pair, LANES)
                return 0

            lax.fori_loop(h * half // LANES, (h + 1) * half // LANES, second, 0)
            for k in order:
                pi, pn = plane_peer(k)
                copy = pltpu.make_async_remote_copy(
                    src_ref=xs.at[g, pi * 2 + pn, :, pl.ds(h * half, half)],
                    dst_ref=back.at[g, mine, :, pl.ds(h * half, half)],
                    send_sem=cs_sem.at[g, h, k], recv_sem=cr_sem.at[g, h, k],
                    device_id=(pi, m, pn), device_id_type=MESH,
                )
                copy.start()
                copies.append(copy)
        here = pltpu.make_async_copy(xs.at[g, mine], back.at[g, mine], copy_sem.at[g, 2])
        here.start()
        sent.extend(copies)
        return copies, here

    def partial(g, which, put):
        weights = pick[g, :, :, block_rows(which)].reshape(total, tok)

        def tile(t, _):
            put(t, lax.dot_general(
                weights, back[g, :, :, lanes(t)].reshape(total, LANES), (((0,), (0,)), ((), ())),
                preferred_element_type=F32,
            ))
            return 0

        lax.fori_loop(0, width // LANES, tile, 0)

    def keep(t, value):
        own[:, lanes(t)] = value

    def partial_to(j, g, which):
        def put(t, value):
            part[j, :, lanes(t)] = value.astype(BF16)

        partial(g, which, put)
        copy = pltpu.make_async_remote_copy(
            src_ref=part.at[j], dst_ref=got.at[j],
            send_sem=ps_sem.at[j], recv_sem=pr_sem.at[j],
            device_id=(i, z_peer(j), n), device_id_type=MESH,
        )
        copy.start()
        sent.append(copy)
        return copy

    def arrive(copies, here):
        for copy in copies:
            copy.wait_recv()
        here.wait()

    loads[0].wait()
    near = [dispatch(0, 0, early_at, early, False)]
    loads[2].wait()
    forward(0)
    block_copies[0].wait_recv()
    near.append(dispatch(0, 1, late_at, late, True))
    forward(1)
    block_copies[1].wait_recv()
    far = [dispatch(1, 0, early_at, early, False)]
    loads[11].wait()
    near_back = backward(0, near)
    block_copies[2].wait_recv()
    far.append(dispatch(1, 1, late_at, late, True))
    far_back = backward(1, far)
    arrive(*near_back)
    ends = [partial_to(1, 0, 1 - zl)]
    partial(0, zl, keep)

    def gradient(t, _):
        out = lax.dot_general(
            hid[...].reshape(2 * total, hidden_width), rows[:, :, :, lanes(t)].reshape(2 * total, LANES),
            (((0,), (0,)), ((), ())), preferred_element_type=F32,
        )
        down_out[:, lanes(t)] = out.astype(BF16)
        return 0

    lax.fori_loop(0, width // LANES, gradient, 0)
    arrive(*far_back)
    ends.append(partial_to(2, 1, zl))
    ends.append(partial_to(3, 1, 1 - zl))
    for copy in ends:
        copy.wait_recv()
    token_out[...] = (
        own[...] + got[1].astype(F32) + got[2].astype(F32) + got[3].astype(F32)
    ).astype(BF16)
    for copy in map_copies + block_copies + sent:
        copy.wait_send()


def fused(out_grad, maps, inputs, gate_up, down, cps):
    tok, width = out_grad.shape
    hidden_width = down.shape[0]
    pair = 2 * cps
    anywhere = pl.BlockSpec(memory_space=pl.ANY)
    local = pl.BlockSpec(memory_space=pltpu.VMEM)
    dma = pltpu.SemaphoreType.DMA
    return pl.pallas_call(
        functools.partial(fused_kernel, cps),
        out_shape=(
            jax.ShapeDtypeStruct((tok, width), BF16),
            jax.ShapeDtypeStruct((hidden_width, width), BF16),
        ),
        in_specs=[anywhere] * 5,
        out_specs=(local, local),
        scratch_shapes=[
            pltpu.VMEM((2, 2 * tok, width), BF16),
            pltpu.VMEM((2, 2, 16, tok), F32),
            pltpu.VMEM((2, 8, pair, 2 * tok), BF16),
            pltpu.VMEM((2, 8, pair, 128), F32),
            pltpu.VMEM((2, 8, pair, width), BF16),
            pltpu.VMEM((2, 8, pair, width), BF16),
            pltpu.VMEM((2, 8, pair, width), BF16),
            pltpu.VMEM((2, 8, pair, width), BF16),
            pltpu.VMEM((2, 4, 4, cps, 2 * hidden_width), F32),
            pltpu.VMEM((width, 2 * hidden_width), BF16),
            pltpu.VMEM((hidden_width, width), BF16),
            pltpu.VMEM((8 * pair, 2 * hidden_width), BF16),
            pltpu.VMEM((2, 8 * pair, hidden_width), BF16),
            pltpu.VMEM((tok, width), F32),
            pltpu.VMEM((4, tok, width), BF16),
            pltpu.VMEM((4, tok, width), BF16),
            dma((12,)), dma((2, 3)), dma((4,)), dma((4,)), dma((4,)), dma((4,)),
            dma((2, 2, 8)), dma((2, 2, 8)), dma((2, 2, 8)), dma((2, 2, 8)), dma((4,)), dma((4,)),
        ],
        compiler_params=pltpu.CompilerParams(
            collective_id=0, has_side_effects=True, vmem_limit_bytes=62 * 1024 * 1024
        ),
    )(out_grad, maps, inputs, gate_up, down)


def routing_maps(ids, gates, count):
    tok = ids.shape[0]
    chosen = ids[:, :, None] == jnp.arange(count, dtype=jnp.int32)
    named = jnp.any(chosen, axis=1)
    before = jnp.arange(tok)[:, None] > jnp.arange(tok)[None, :]
    slot = jnp.dot(
        before.astype(jnp.bfloat16), named.astype(jnp.bfloat16), preferred_element_type=jnp.float32
    )
    slot = jnp.where(named, slot, -1024.0)
    gate = jnp.sum(jnp.where(chosen, gates[:, :, None], 0.0), axis=1)
    return slot.T, gate.T


def per_device(out_grad, expert_ids, gates, expert_input, gate_up_weight, down_weight):
    inner, major, minor = lax.axis_size("i"), lax.axis_size("m"), lax.axis_size("n")
    plane = inner * minor
    tok = expert_ids.shape[0]
    sources, _, cps, width = expert_input.shape
    slot, gate = routing_maps(expert_ids, gates, sources)
    if (inner, major, minor, tok, cps % 8) == (4, 4, 2, 128, 0):
        maps = jnp.stack([slot, gate]).reshape(2, inner, major, minor, tok).transpose(2, 0, 1, 3, 4)
        token_grad, down_grad = fused(
            out_grad, maps.reshape(major, 2 * plane, tok),
            expert_input.reshape(inner, major, minor * cps, width), gate_up_weight[0], down_weight[0], cps,
        )
        return token_grad, down_grad[None]
    maps = jnp.stack([slot, gate]).reshape(2, inner, major, minor, tok).transpose(2, 0, 1, 3, 4)
    maps = lax.all_to_all(maps, "m", split_axis=0, concat_axis=0, tiled=True)
    slot, gate = maps[:, 0].reshape(major, plane, tok), maps[:, 1].reshape(major, plane, tok)
    blocks = lax.all_gather(out_grad, "m")
    pick = slot[:, :, None, :] == jnp.arange(cps, dtype=jnp.float32)[:, None]
    scale = jnp.sum(jnp.where(pick, gate[:, :, None, :], 0.0), axis=-1)
    pick = pick.astype(jnp.bfloat16)
    rows = jnp.einsum("mpct,mtd->pmcd", pick, blocks, preferred_element_type=jnp.float32)
    rows = (rows * scale.transpose(1, 0, 2)[..., None]).astype(jnp.bfloat16)
    rows = lax.all_to_all(rows, PLANE, split_axis=0, concat_axis=0, tiled=True)
    rows = rows.reshape(sources * cps, width)
    inputs = expert_input.reshape(inner, major, minor, cps, width).transpose(0, 2, 1, 3, 4)
    inputs = inputs.reshape(sources * cps, width)

    gate_up, down = gate_up_weight[0], down_weight[0]
    hidden_width = down.shape[0]
    pre = jnp.dot(inputs, gate_up, preferred_element_type=jnp.float32)
    act_a, act_b = pre[:, :hidden_width], pre[:, hidden_width:]
    sigma = jax.nn.sigmoid(act_a)
    silu_a = act_a * sigma
    hidden = (silu_a * act_b).astype(jnp.bfloat16)
    grad_h = lax.dot_general(
        rows, down, (((1,), (1,)), ((), ())), preferred_element_type=jnp.float32
    )
    grad_a = grad_h * act_b * sigma * (1.0 + act_a * (1.0 - sigma))
    grad_gu = jnp.concatenate([grad_a, grad_h * silu_a], axis=1).astype(jnp.bfloat16)
    slot_grad = lax.dot_general(
        grad_gu, gate_up, (((1,), (1,)), ((), ())), preferred_element_type=jnp.float32
    ).astype(jnp.bfloat16)
    down_grad = lax.dot_general(
        hidden, rows, (((0,), (0,)), ((), ())), preferred_element_type=jnp.float32
    ).astype(jnp.bfloat16)

    back = slot_grad.reshape(plane, major, cps, width)
    back = lax.all_to_all(back, PLANE, split_axis=0, concat_axis=0, tiled=True)
    part = jnp.einsum("mpct,pmcd->mtd", pick, back, preferred_element_type=jnp.float32)
    part = part.astype(jnp.bfloat16)
    part = lax.all_to_all(part, "m", split_axis=0, concat_axis=0, tiled=True)
    token_grad = jnp.sum(part.astype(jnp.float32), axis=0).astype(jnp.bfloat16)
    return token_grad, down_grad[None]


def solution(mesh):
    inner, outer = mesh.devices.shape
    major = 4
    fine = Mesh(mesh.devices.reshape(inner, major, outer // major), ("i", "m", "n"))
    every = ("i", "m", "n")
    placed = (
        P(every, None),
        P(every, None),
        P(every, None),
        P(None, every, None, None),
        P(every, None, None),
        P(every, None, None),
    )
    return jax.shard_map(
        per_device,
        mesh=fine,
        in_specs=placed,
        out_specs=(P(every, None), P(every, None, None)),
        check_vma=False,
    )
```

```python
import functools

import jax
import jax.numpy as jnp
from jax import lax
from jax.experimental import pallas as pl
from jax.experimental.pallas import tpu as pltpu
from jax.sharding import Mesh, PartitionSpec as P

PLANE = ("i", "n")
MESH = pl.DeviceIdType.MESH
F32, BF16 = jnp.float32, jnp.bfloat16
LANES = 512


def fused_kernel(
    cps, og_in, maps_in, x_in, wgu_in, wd_in, token_out, down_out,
    og, maps, pick, scale, send, rows, xs, back, pre, wgu, wd, dgu, hid, own, hold, part, got,
    load_sem, copy_sem, zs_sem, zr_sem, ms_sem, mr_sem, ds_sem, dr_sem, cs_sem, cr_sem, ps_sem, pr_sem,
):
    i, m, n = lax.axis_index("i"), lax.axis_index("m"), lax.axis_index("n")
    x, c = i // 2, i % 2
    zh, zl = m // 2, m % 2
    mine = i * 2 + n
    tok, width = og_in.shape
    hidden_width = wd_in.shape[0]
    pair = 2 * cps
    total = 8 * pair
    early = cps // 16 * 16
    late = pair - early
    early_at = pl.multiple_of(zl * late, 16)
    late_at = pl.multiple_of((1 - zl) * early, 16)

    def z_peer(j):
        return 2 * ((zh + j // 2) % 2) + (zl + j % 2) % 2

    def plane_peer(k):
        ki, kc, kn = k // 4, k // 2 % 2, k % 2
        return 2 * ((x + ki) % 2) + (c + kc) % 2, (n + kn) % 2

    def block_rows(which):
        return pl.ds(pl.multiple_of(which * tok, tok), tok)

    loads = [
        pltpu.make_async_copy(og_in, og.at[0, block_rows(zl)], load_sem.at[0]),
        pltpu.make_async_copy(maps_in.at[m], maps.at[0, zl], load_sem.at[1]),
        pltpu.make_async_copy(wgu_in, wgu, load_sem.at[2]),
    ]
    for g in range(2):
        for a in range(4):
            loads.append(
                pltpu.make_async_copy(
                    x_in.at[a, pl.ds(2 * ((zh + g) % 2), 2)],
                    xs.at[g, pl.ds(2 * a, 2)],
                    load_sem.at[3 + 4 * g + a],
                )
            )
    loads.append(pltpu.make_async_copy(wd_in, wd, load_sem.at[11]))
    for load in loads:
        load.start()

    barrier = pltpu.get_barrier_semaphore()
    for j in range(1, 4):
        pl.semaphore_signal(barrier, inc=1, device_id=(i, z_peer(j), n), device_id_type=MESH)
    for k in range(1, 8):
        pi, pn = plane_peer(k)
        pl.semaphore_signal(barrier, inc=1, device_id=(pi, m, pn), device_id_type=MESH)
    pl.semaphore_wait(barrier, 10)

    map_copies, block_copies = [], []
    for j in range(1, 4):
        there = z_peer(j)
        map_copies.append(
            pltpu.make_async_remote_copy(
                src_ref=maps_in.at[there], dst_ref=maps.at[j // 2, zl],
                send_sem=ms_sem.at[j], recv_sem=mr_sem.at[j],
                device_id=(i, there, n), device_id_type=MESH,
            )
        )
        block_copies.append(
            pltpu.make_async_remote_copy(
                src_ref=og.at[1, block_rows(zl)] if j == 3 else og_in, dst_ref=og.at[j // 2, block_rows(zl)],
                send_sem=zs_sem.at[j], recv_sem=zr_sem.at[j],
                device_id=(i, z_peer(j % 2 or 2), n), device_id_type=MESH,
            )
        )
    near_copy, cross_copy, forward_copy = block_copies
    for copy in map_copies:
        copy.start()
    near_copy.start()

    @pl.when(zh + zl == 1)
    def _():
        cross_copy.start()

    loads[1].wait()
    for copy in map_copies:
        copy.wait_recv()
    place = lax.broadcasted_iota(jnp.int32, (pair, 2 * tok), 0).astype(F32)
    for g in range(2):
        for p in range(8):
            slot = jnp.concatenate([maps[g, 0, p : p + 1, :], maps[g, 1, p : p + 1, :] + cps], axis=1)
            gate = jnp.concatenate([maps[g, 0, 8 + p : 9 + p, :], maps[g, 1, 8 + p : 9 + p, :]], axis=1)
            hit = place == slot
            pick[g, p] = jnp.where(hit, 1.0, 0.0).astype(BF16)
            factor = jnp.sum(jnp.where(hit, gate, 0.0), axis=1, keepdims=True)
            scale[g, p] = jnp.broadcast_to(factor, (pair, 128))

    def lanes(t, size=LANES):
        return pl.ds(pl.multiple_of(t * size, size), size)

    order = (5, 7, 4, 1, 6, 3, 2)
    sent = []
    half = width // 2

    def dispatch(g, chunk, start, size, whole):
        tokens = slice(None) if whole else block_rows(zl)
        depth = 2 * tok if whole else tok
        weights = pick[g, :, pl.ds(start, size), tokens].reshape(8 * size, depth)
        factor = scale[g, :, pl.ds(start, size), :].reshape(8 * size, 128)[:, :1]

        def tile(t, _):
            out = jnp.dot(weights, og[g, tokens, lanes(t)], preferred_element_type=F32) * factor
            send[g, :, pl.ds(start, size), lanes(t)] = out.astype(BF16).reshape(8, size, LANES)
            return 0

        lax.fori_loop(0, width // LANES, tile, 0)
        copies = []
        for k in order:
            pi, pn = plane_peer(k)
            copy = pltpu.make_async_remote_copy(
                src_ref=send.at[g, pi * 2 + pn, pl.ds(start, size)],
                dst_ref=rows.at[g, mine, pl.ds(start, size)],
                send_sem=ds_sem.at[g, chunk, k], recv_sem=dr_sem.at[g, chunk, k],
                device_id=(pi, m, pn), device_id_type=MESH,
            )
            copy.start()
            copies.append(copy)
        here = pltpu.make_async_copy(
            send.at[g, mine, pl.ds(start, size)], rows.at[g, mine, pl.ds(start, size)], copy_sem.at[g, chunk]
        )
        here.start()
        sent.extend(copies)
        return copies, here

    def forward(g):
        for a in range(4):
            loads[3 + 4 * g + a].wait()

        def tile(t, _):
            out = jnp.dot(
                xs[g].reshape(total, width), wgu[:, lanes(t)], preferred_element_type=F32
            ).reshape(4, 4, cps, LANES)
            for a in range(2):
                for b in range(2):
                    pre[g, :, b * 2 + a, :, lanes(t)] = out[:, a * 2 + b]
            return 0

        lax.fori_loop(0, 2 * hidden_width // LANES, tile, 0)

    def backward(g, arriving, go):
        for copies, here in arriving:
            for copy in copies:
                copy.wait_recv()
            here.wait()

        def first(t, _):
            size = 256
            at_b = pl.ds(pl.multiple_of(hidden_width + t * size, size), size)
            grad_h = lax.dot_general(
                rows[g].reshape(total, width), wd[lanes(t, size), :], (((1,), (1,)), ((), ())),
                preferred_element_type=F32,
            )
            act_a = pre[g, :, :, :, lanes(t, size)].reshape(total, size)
            act_b = pre[g, :, :, :, at_b].reshape(total, size)
            sigma = jax.nn.sigmoid(act_a)
            silu_a = act_a * sigma
            hid[g, :, lanes(t, size)] = (silu_a * act_b).astype(BF16)
            dgu[:, lanes(t, size)] = (
                grad_h * act_b * sigma * (1.0 + act_a * (1.0 - sigma))
            ).astype(BF16)
            dgu[:, at_b] = (grad_h * silu_a).astype(BF16)
            return 0

        lax.fori_loop(0, hidden_width // 256, first, 0)
        copies = []
        for h in range(2):
            def second(t, _):
                out = lax.dot_general(
                    dgu[...], wgu[lanes(t), :], (((1,), (1,)), ((), ())), preferred_element_type=F32
                )
                xs[g, :, :, lanes(t)] = out.astype(BF16).reshape(8, pair, LANES)
                return 0

            lax.fori_loop(h * half // LANES, (h + 1) * half // LANES, second, 0)
            if go:
                copies.append(hand_back(g, h))
        return copies

    def hand_back(g, h):
        cols = pl.ds(h * half, half)
        copies = []
        for k in order:
            pi, pn = plane_peer(k)
            copy = pltpu.make_async_remote_copy(
                src_ref=xs.at[g, pi * 2 + pn, :, cols], dst_ref=back.at[g, mine, :, cols],
                send_sem=cs_sem.at[g, h, k], recv_sem=cr_sem.at[g, h, k],
                device_id=(pi, m, pn), device_id_type=MESH,
            )
            copy.start()
            copies.append(copy)
        here = pltpu.make_async_copy(xs.at[g, mine, :, cols], back.at[g, mine, :, cols], copy_sem.at[g, 2 + h])
        here.start()
        sent.extend(copies)
        return copies, here

    def partial(g, which, h, put):
        weights = pick[g, :, :, block_rows(which)].reshape(total, tok)

        def tile(t, _):
            put(t, lax.dot_general(
                weights, back[g, :, :, lanes(t)].reshape(total, LANES), (((0,), (0,)), ((), ())),
                preferred_element_type=F32,
            ))
            return 0

        lax.fori_loop(h * half // LANES, (h + 1) * half // LANES, tile, 0)

    def keep(t, value):
        own[:, lanes(t)] = value

    def set_aside(t, value):
        hold[:, lanes(t)] = value

    def ship(j, h, to):
        cols = pl.ds(h * half, half)
        copy = pltpu.make_async_remote_copy(
            src_ref=part.at[j, :, cols], dst_ref=got.at[j, :, cols],
            send_sem=ps_sem.at[j, h], recv_sem=pr_sem.at[j, h],
            device_id=(i, z_peer(to), n), device_id_type=MESH,
        )
        copy.start()
        sent.append(copy)
        return copy

    def near_part(h, arriving):
        arrive(*arriving)

        def put(t, value):
            part[1, :, lanes(t)] = value.astype(BF16)

        partial(0, 1 - zl, h, put)
        copy = ship(1, h, 1)
        partial(0, zl, h, keep)
        return copy

    def far_part(h, arriving):
        arrive(*arriving)

        def put(t, value):
            part[3, :, lanes(t)] = value.astype(BF16)

        partial(1, 1 - zl, h, put)
        copy = ship(3, h, 1)
        partial(1, zl, h, set_aside)
        copy.wait_recv()
        cols = pl.ds(h * half, half)
        part[2, :, cols] = (hold[:, cols] + got[3, :, cols].astype(F32)).astype(BF16)
        return ship(2, h, 2)

    def arrive(copies, here):
        for copy in copies:
            copy.wait_recv()
        here.wait()

    loads[0].wait()
    near = [dispatch(0, 0, early_at, early, False)]
    loads[2].wait()
    forward(0)
    near_copy.wait_send()

    @pl.when(zh + zl != 1)
    def _():
        cross_copy.start()

    near_copy.wait_recv()
    near.append(dispatch(0, 1, late_at, late, True))
    forward(1)
    cross_copy.wait_recv()
    forward_copy.start()
    far = [dispatch(1, 0, early_at, early, False)]
    loads[11].wait()
    backward(0, near, False)
    forward_copy.wait_recv()
    far.append(dispatch(1, 1, late_at, late, True))
    near_back = [hand_back(0, 0)]
    far_back = backward(1, far, True)
    near_back.append(hand_back(0, 1))
    ends = [near_part(0, near_back[0])]

    def gradient(t, _):
        out = lax.dot_general(
            hid[...].reshape(2 * total, hidden_width), rows[:, :, :, lanes(t)].reshape(2 * total, LANES),
            (((0,), (0,)), ((), ())), preferred_element_type=F32,
        )
        down_out[:, lanes(t)] = out.astype(BF16)
        return 0

    lax.fori_loop(0, width // LANES, gradient, 0)
    ends.append(far_part(0, far_back[0]))
    ends.append(far_part(1, far_back[1]))
    ends.append(near_part(1, near_back[1]))
    for copy in ends:
        copy.wait_recv()
    token_out[...] = (
        own[...] + got[1].astype(F32) + got[2].astype(F32)
    ).astype(BF16)
    for copy in map_copies + [cross_copy, forward_copy] + sent:
        copy.wait_send()


def fused(out_grad, maps, inputs, gate_up, down, cps):
    tok, width = out_grad.shape
    hidden_width = down.shape[0]
    pair = 2 * cps
    anywhere = pl.BlockSpec(memory_space=pl.ANY)
    local = pl.BlockSpec(memory_space=pltpu.VMEM)
    dma = pltpu.SemaphoreType.DMA
    return pl.pallas_call(
        functools.partial(fused_kernel, cps),
        out_shape=(
            jax.ShapeDtypeStruct((tok, width), BF16),
            jax.ShapeDtypeStruct((hidden_width, width), BF16),
        ),
        in_specs=[anywhere] * 5,
        out_specs=(local, local),
        scratch_shapes=[
            pltpu.VMEM((2, 2 * tok, width), BF16),
            pltpu.VMEM((2, 2, 16, tok), F32),
            pltpu.VMEM((2, 8, pair, 2 * tok), BF16),
            pltpu.VMEM((2, 8, pair, 128), F32),
            pltpu.VMEM((2, 8, pair, width), BF16),
            pltpu.VMEM((2, 8, pair, width), BF16),
            pltpu.VMEM((2, 8, pair, width), BF16),
            pltpu.VMEM((2, 8, pair, width), BF16),
            pltpu.VMEM((2, 4, 4, cps, 2 * hidden_width), F32),
            pltpu.VMEM((width, 2 * hidden_width), BF16),
            pltpu.VMEM((hidden_width, width), BF16),
            pltpu.VMEM((8 * pair, 2 * hidden_width), BF16),
            pltpu.VMEM((2, 8 * pair, hidden_width), BF16),
            pltpu.VMEM((tok, width), F32),
            pltpu.VMEM((tok, width), F32),
            pltpu.VMEM((4, tok, width), BF16),
            pltpu.VMEM((4, tok, width), BF16),
            dma((12,)), dma((2, 4)), dma((4,)), dma((4,)), dma((4,)), dma((4,)),
            dma((2, 2, 8)), dma((2, 2, 8)), dma((2, 2, 8)), dma((2, 2, 8)), dma((4, 2)), dma((4, 2)),
        ],
        compiler_params=pltpu.CompilerParams(
            collective_id=0, has_side_effects=True, vmem_limit_bytes=62 * 1024 * 1024
        ),
    )(out_grad, maps, inputs, gate_up, down)


def routing_maps(ids, gates, count):
    tok = ids.shape[0]
    chosen = ids[:, :, None] == jnp.arange(count, dtype=jnp.int32)
    named = jnp.any(chosen, axis=1)
    before = jnp.arange(tok)[:, None] > jnp.arange(tok)[None, :]
    slot = jnp.dot(
        before.astype(jnp.bfloat16), named.astype(jnp.bfloat16), preferred_element_type=jnp.float32
    )
    slot = jnp.where(named, slot, -1024.0)
    gate = jnp.sum(jnp.where(chosen, gates[:, :, None], 0.0), axis=1)
    return slot.T, gate.T


def per_device(out_grad, expert_ids, gates, expert_input, gate_up_weight, down_weight):
    inner, major, minor = lax.axis_size("i"), lax.axis_size("m"), lax.axis_size("n")
    plane = inner * minor
    tok = expert_ids.shape[0]
    sources, _, cps, width = expert_input.shape
    slot, gate = routing_maps(expert_ids, gates, sources)
    if (inner, major, minor, tok, cps % 8) == (4, 4, 2, 128, 0):
        maps = jnp.stack([slot, gate]).reshape(2, inner, major, minor, tok).transpose(2, 0, 1, 3, 4)
        token_grad, down_grad = fused(
            out_grad, maps.reshape(major, 2 * plane, tok),
            expert_input.reshape(inner, major, minor * cps, width), gate_up_weight[0], down_weight[0], cps,
        )
        return token_grad, down_grad[None]
    maps = jnp.stack([slot, gate]).reshape(2, inner, major, minor, tok).transpose(2, 0, 1, 3, 4)
    maps = lax.all_to_all(maps, "m", split_axis=0, concat_axis=0, tiled=True)
    slot, gate = maps[:, 0].reshape(major, plane, tok), maps[:, 1].reshape(major, plane, tok)
    blocks = lax.all_gather(out_grad, "m")
    pick = slot[:, :, None, :] == jnp.arange(cps, dtype=jnp.float32)[:, None]
    scale = jnp.sum(jnp.where(pick, gate[:, :, None, :], 0.0), axis=-1)
    pick = pick.astype(jnp.bfloat16)
    rows = jnp.einsum("mpct,mtd->pmcd", pick, blocks, preferred_element_type=jnp.float32)
    rows = (rows * scale.transpose(1, 0, 2)[..., None]).astype(jnp.bfloat16)
    rows = lax.all_to_all(rows, PLANE, split_axis=0, concat_axis=0, tiled=True)
    rows = rows.reshape(sources * cps, width)
    inputs = expert_input.reshape(inner, major, minor, cps, width).transpose(0, 2, 1, 3, 4)
    inputs = inputs.reshape(sources * cps, width)

    gate_up, down = gate_up_weight[0], down_weight[0]
    hidden_width = down.shape[0]
    pre = jnp.dot(inputs, gate_up, preferred_element_type=jnp.float32)
    act_a, act_b = pre[:, :hidden_width], pre[:, hidden_width:]
    sigma = jax.nn.sigmoid(act_a)
    silu_a = act_a * sigma
    hidden = (silu_a * act_b).astype(jnp.bfloat16)
    grad_h = lax.dot_general(
        rows, down, (((1,), (1,)), ((), ())), preferred_element_type=jnp.float32
    )
    grad_a = grad_h * act_b * sigma * (1.0 + act_a * (1.0 - sigma))
    grad_gu = jnp.concatenate([grad_a, grad_h * silu_a], axis=1).astype(jnp.bfloat16)
    slot_grad = lax.dot_general(
        grad_gu, gate_up, (((1,), (1,)), ((), ())), preferred_element_type=jnp.float32
    ).astype(jnp.bfloat16)
    down_grad = lax.dot_general(
        hidden, rows, (((0,), (0,)), ((), ())), preferred_element_type=jnp.float32
    ).astype(jnp.bfloat16)

    back = slot_grad.reshape(plane, major, cps, width)
    back = lax.all_to_all(back, PLANE, split_axis=0, concat_axis=0, tiled=True)
    part = jnp.einsum("mpct,pmcd->mtd", pick, back, preferred_element_type=jnp.float32)
    part = part.astype(jnp.bfloat16)
    part = lax.all_to_all(part, "m", split_axis=0, concat_axis=0, tiled=True)
    token_grad = jnp.sum(part.astype(jnp.float32), axis=0).astype(jnp.bfloat16)
    return token_grad, down_grad[None]


def solution(mesh):
    inner, outer = mesh.devices.shape
    major = 4
    fine = Mesh(mesh.devices.reshape(inner, major, outer // major), ("i", "m", "n"))
    every = ("i", "m", "n")
    placed = (
        P(every, None),
        P(every, None),
        P(every, None),
        P(None, every, None, None),
        P(every, None, None),
        P(every, None, None),
    )
    return jax.shard_map(
        per_device,
        mesh=fine,
        in_specs=placed,
        out_specs=(P(every, None), P(every, None, None)),
        check_vma=False,
    )
```

```python
import functools

import jax
import jax.numpy as jnp
from jax import lax
from jax.experimental import pallas as pl
from jax.experimental.pallas import tpu as pltpu
from jax.sharding import Mesh, PartitionSpec as P

PLANE = ("i", "n")
MESH = pl.DeviceIdType.MESH
F32, BF16 = jnp.float32, jnp.bfloat16
LANES = 512


def fused_kernel(
    cps, og_in, maps_in, x_in, wgu_in, wd_in, token_out, down_out,
    og, maps, pick, scale, send, rows, xs, back, pre, wgu, wd, dgu, hid, down, own, hold, part, got,
    load_sem, copy_sem, zs_sem, zr_sem, ms_sem, mr_sem, ds_sem, dr_sem, cs_sem, cr_sem, ps_sem, pr_sem,
):
    i, m, n = lax.axis_index("i"), lax.axis_index("m"), lax.axis_index("n")
    x, c = i // 2, i % 2
    zh, zl = m // 2, m % 2
    mine = i * 2 + n
    tok, width = og_in.shape
    hidden_width = wd_in.shape[0]
    pair = 2 * cps
    total = 8 * pair
    early = cps // 16 * 16
    late = pair - early
    early_at = pl.multiple_of(zl * late, 16)
    late_at = pl.multiple_of((1 - zl) * early, 16)

    def z_peer(j):
        return 2 * ((zh + j // 2) % 2) + (zl + j % 2) % 2

    def plane_peer(k):
        ki, kc, kn = k // 4, k // 2 % 2, k % 2
        return 2 * ((x + ki) % 2) + (c + kc) % 2, (n + kn) % 2

    def block_rows(which):
        return pl.ds(pl.multiple_of(which * tok, tok), tok)

    loads = [
        pltpu.make_async_copy(og_in, og.at[0, block_rows(zl)], load_sem.at[0]),
        pltpu.make_async_copy(maps_in.at[m], maps.at[0, zl], load_sem.at[1]),
        pltpu.make_async_copy(wgu_in, wgu, load_sem.at[2]),
    ]
    for g in range(2):
        for a in range(4):
            loads.append(
                pltpu.make_async_copy(
                    x_in.at[a, pl.ds(2 * ((zh + g) % 2), 2)],
                    xs.at[g, pl.ds(2 * a, 2)],
                    load_sem.at[3 + 4 * g + a],
                )
            )
    loads.append(pltpu.make_async_copy(wd_in, wd, load_sem.at[11]))
    for load in loads:
        load.start()

    barrier = pltpu.get_barrier_semaphore()
    for j in range(1, 4):
        pl.semaphore_signal(barrier, inc=1, device_id=(i, z_peer(j), n), device_id_type=MESH)
    for k in range(1, 8):
        pi, pn = plane_peer(k)
        pl.semaphore_signal(barrier, inc=1, device_id=(pi, m, pn), device_id_type=MESH)

    place = lax.broadcasted_iota(jnp.int32, (pair, tok), 0).astype(F32)

    def choose(g, which, first):
        for p in range(8):
            hit = place == maps[g, which, p : p + 1, :] + (cps * which).astype(F32)
            pick[g, p, :, block_rows(which)] = jnp.where(hit, 1.0, 0.0).astype(BF16)
            factor = jnp.sum(jnp.where(hit, maps[g, which, 8 + p : 9 + p, :], 0.0), axis=1, keepdims=True)
            factor = jnp.broadcast_to(factor, (pair, 128))
            scale[g, p] = factor if first else scale[g, p] + factor

    loads[1].wait()
    choose(0, zl, True)
    pl.semaphore_wait(barrier, 10)

    map_copies, block_copies = [], []
    for j in range(1, 4):
        there = z_peer(j)
        map_copies.append(
            pltpu.make_async_remote_copy(
                src_ref=maps_in.at[there], dst_ref=maps.at[j // 2, zl],
                send_sem=ms_sem.at[j], recv_sem=mr_sem.at[j],
                device_id=(i, there, n), device_id_type=MESH,
            )
        )
        block_copies.append(
            pltpu.make_async_remote_copy(
                src_ref=og.at[1, block_rows(zl)] if j == 3 else og_in, dst_ref=og.at[j // 2, block_rows(zl)],
                send_sem=zs_sem.at[j], recv_sem=zr_sem.at[j],
                device_id=(i, z_peer(j % 2 or 2), n), device_id_type=MESH,
            )
        )
    near_copy, cross_copy, forward_copy = block_copies
    for copy in map_copies:
        copy.start()
    near_copy.start()

    @pl.when(zh + zl == 1)
    def _():
        cross_copy.start()

    def lanes(t, size=LANES):
        return pl.ds(pl.multiple_of(t * size, size), size)

    order = (5, 7, 4, 1, 6, 3, 2)
    sent = []
    half = width // 2

    def dispatch(g, chunk, start, size, whole):
        tokens = slice(None) if whole else block_rows(zl)
        depth = 2 * tok if whole else tok
        weights = pick[g, :, pl.ds(start, size), tokens].reshape(8 * size, depth)
        factor = scale[g, :, pl.ds(start, size), :].reshape(8 * size, 128)[:, :1]

        def tile(t, _):
            out = jnp.dot(weights, og[g, tokens, lanes(t)], preferred_element_type=F32) * factor
            send[g, :, pl.ds(start, size), lanes(t)] = out.astype(BF16).reshape(8, size, LANES)
            return 0

        lax.fori_loop(0, width // LANES, tile, 0)
        copies = []
        for k in order:
            pi, pn = plane_peer(k)
            copy = pltpu.make_async_remote_copy(
                src_ref=send.at[g, pi * 2 + pn, pl.ds(start, size)],
                dst_ref=rows.at[g, mine, pl.ds(start, size)],
                send_sem=ds_sem.at[g, chunk, k], recv_sem=dr_sem.at[g, chunk, k],
                device_id=(pi, m, pn), device_id_type=MESH,
            )
            copy.start()
            copies.append(copy)
        here = pltpu.make_async_copy(
            send.at[g, mine, pl.ds(start, size)], rows.at[g, mine, pl.ds(start, size)], copy_sem.at[g, chunk]
        )
        here.start()
        sent.extend(copies)
        return copies, here

    def forward(g):
        for a in range(4):
            loads[3 + 4 * g + a].wait()

        def tile(t, _):
            out = jnp.dot(
                xs[g].reshape(total, width), wgu[:, lanes(t)], preferred_element_type=F32
            ).reshape(4, 4, cps, LANES)
            for a in range(2):
                for b in range(2):
                    pre[g, :, b * 2 + a, :, lanes(t)] = out[:, a * 2 + b]
            return 0

        lax.fori_loop(0, 2 * hidden_width // LANES, tile, 0)

    def backward(g, arriving, go):
        for copies, here in arriving:
            for copy in copies:
                copy.wait_recv()
            here.wait()

        def first(t, _):
            size = 256
            at_b = pl.ds(pl.multiple_of(hidden_width + t * size, size), size)
            grad_h = lax.dot_general(
                rows[g].reshape(total, width), wd[lanes(t, size), :], (((1,), (1,)), ((), ())),
                preferred_element_type=F32,
            )
            act_a = pre[g, :, :, :, lanes(t, size)].reshape(total, size)
            act_b = pre[g, :, :, :, at_b].reshape(total, size)
            sigma = jax.nn.sigmoid(act_a)
            silu_a = act_a * sigma
            hid[g, :, lanes(t, size)] = (silu_a * act_b).astype(BF16)
            dgu[:, lanes(t, size)] = (
                grad_h * act_b * sigma * (1.0 + act_a * (1.0 - sigma))
            ).astype(BF16)
            dgu[:, at_b] = (grad_h * silu_a).astype(BF16)
            return 0

        lax.fori_loop(0, hidden_width // 256, first, 0)
        copies = []
        for h in range(2):
            def second(t, _):
                out = lax.dot_general(
                    dgu[...], wgu[lanes(t), :], (((1,), (1,)), ((), ())), preferred_element_type=F32
                )
                xs[g, :, :, lanes(t)] = out.astype(BF16).reshape(8, pair, LANES)
                return 0

            lax.fori_loop(h * half // LANES, (h + 1) * half // LANES, second, 0)
            if go:
                copies.append(hand_back(g, h))
        return copies

    def hand_back(g, h):
        cols = pl.ds(h * half, half)
        copies = []
        for k in order:
            pi, pn = plane_peer(k)
            copy = pltpu.make_async_remote_copy(
                src_ref=xs.at[g, pi * 2 + pn, :, cols], dst_ref=back.at[g, mine, :, cols],
                send_sem=cs_sem.at[g, h, k], recv_sem=cr_sem.at[g, h, k],
                device_id=(pi, m, pn), device_id_type=MESH,
            )
            copy.start()
            copies.append(copy)
        here = pltpu.make_async_copy(xs.at[g, mine, :, cols], back.at[g, mine, :, cols], copy_sem.at[g, 2 + h])
        here.start()
        sent.extend(copies)
        return copies, here

    def partial(g, which, h, put):
        weights = pick[g, :, :, block_rows(which)].reshape(total, tok)

        def tile(t, _):
            put(t, lax.dot_general(
                weights, back[g, :, :, lanes(t)].reshape(total, LANES), (((0,), (0,)), ((), ())),
                preferred_element_type=F32,
            ))
            return 0

        lax.fori_loop(h * half // LANES, (h + 1) * half // LANES, tile, 0)

    def keep(t, value):
        own[:, lanes(t)] = value

    def set_aside(t, value):
        hold[:, lanes(t)] = value

    def ship(j, h, to):
        cols = pl.ds(h * half, half)
        copy = pltpu.make_async_remote_copy(
            src_ref=part.at[j, :, cols], dst_ref=got.at[j, :, cols],
            send_sem=ps_sem.at[j, h], recv_sem=pr_sem.at[j, h],
            device_id=(i, z_peer(to), n), device_id_type=MESH,
        )
        copy.start()
        sent.append(copy)
        return copy

    def near_part(h, arriving):
        arrive(*arriving)

        def put(t, value):
            part[1, :, lanes(t)] = value.astype(BF16)

        partial(0, 1 - zl, h, put)
        copy = ship(1, h, 1)
        partial(0, zl, h, keep)
        return copy

    def far_part(h, arriving):
        arrive(*arriving)

        def put(t, value):
            part[3, :, lanes(t)] = value.astype(BF16)

        partial(1, 1 - zl, h, put)
        copy = ship(3, h, 1)
        partial(1, zl, h, set_aside)
        copy.wait_recv()
        cols = pl.ds(h * half, half)
        part[2, :, cols] = (hold[:, cols] + got[3, :, cols].astype(F32)).astype(BF16)
        return ship(2, h, 2)

    def arrive(copies, here):
        for copy in copies:
            copy.wait_recv()
        here.wait()

    loads[0].wait()
    near = [dispatch(0, 0, early_at, early, False)]
    for copy in map_copies:
        copy.wait_recv()
    choose(0, 1 - zl, False)
    choose(1, zl, True)
    choose(1, 1 - zl, False)
    loads[2].wait()
    forward(0)
    near_copy.wait_send()

    @pl.when(zh + zl != 1)
    def _():
        cross_copy.start()

    near_copy.wait_recv()
    near.append(dispatch(0, 1, late_at, late, True))
    forward(1)
    cross_copy.wait_recv()
    forward_copy.start()
    far = [dispatch(1, 0, early_at, early, False)]
    loads[11].wait()
    forward_copy.wait_recv()
    far.append(dispatch(1, 1, late_at, late, True))
    backward(0, near, False)
    near_back = [hand_back(0, 0)]
    far_back = backward(1, far, True)
    near_back.append(hand_back(0, 1))
    def gradient(t, _):
        out = lax.dot_general(
            hid[...].reshape(2 * total, hidden_width), rows[:, :, :, lanes(t)].reshape(2 * total, LANES),
            (((0,), (0,)), ((), ())), preferred_element_type=F32,
        )
        down[:, lanes(t)] = out.astype(BF16)
        return 0

    lax.fori_loop(0, width // LANES, gradient, 0)
    result = pltpu.make_async_copy(down, down_out, load_sem.at[12])
    result.start()
    ends = [near_part(0, near_back[0])]
    ends.append(far_part(0, far_back[0]))
    ends.append(far_part(1, far_back[1]))
    ends.append(near_part(1, near_back[1]))
    for copy in ends:
        copy.wait_recv()
    token_out[...] = (
        own[...] + got[1].astype(F32) + got[2].astype(F32)
    ).astype(BF16)
    result.wait()
    for copy in map_copies + [cross_copy, forward_copy] + sent:
        copy.wait_send()


def fused(out_grad, maps, inputs, gate_up, down, cps):
    tok, width = out_grad.shape
    hidden_width = down.shape[0]
    pair = 2 * cps
    anywhere = pl.BlockSpec(memory_space=pl.ANY)
    local = pl.BlockSpec(memory_space=pltpu.VMEM)
    dma = pltpu.SemaphoreType.DMA
    return pl.pallas_call(
        functools.partial(fused_kernel, cps),
        out_shape=(
            jax.ShapeDtypeStruct((tok, width), BF16),
            jax.ShapeDtypeStruct((hidden_width, width), BF16),
        ),
        in_specs=[anywhere] * 5,
        out_specs=(local, anywhere),
        scratch_shapes=[
            pltpu.VMEM((2, 2 * tok, width), BF16),
            pltpu.VMEM((2, 2, 16, tok), F32),
            pltpu.VMEM((2, 8, pair, 2 * tok), BF16),
            pltpu.VMEM((2, 8, pair, 128), F32),
            pltpu.VMEM((2, 8, pair, width), BF16),
            pltpu.VMEM((2, 8, pair, width), BF16),
            pltpu.VMEM((2, 8, pair, width), BF16),
            pltpu.VMEM((2, 8, pair, width), BF16),
            pltpu.VMEM((2, 4, 4, cps, 2 * hidden_width), F32),
            pltpu.VMEM((width, 2 * hidden_width), BF16),
            pltpu.VMEM((hidden_width, width), BF16),
            pltpu.VMEM((8 * pair, 2 * hidden_width), BF16),
            pltpu.VMEM((2, 8 * pair, hidden_width), BF16),
            pltpu.VMEM((hidden_width, width), BF16),
            pltpu.VMEM((tok, width), F32),
            pltpu.VMEM((tok, width), F32),
            pltpu.VMEM((4, tok, width), BF16),
            pltpu.VMEM((4, tok, width), BF16),
            dma((13,)), dma((2, 4)), dma((4,)), dma((4,)), dma((4,)), dma((4,)),
            dma((2, 2, 8)), dma((2, 2, 8)), dma((2, 2, 8)), dma((2, 2, 8)), dma((4, 2)), dma((4, 2)),
        ],
        compiler_params=pltpu.CompilerParams(
            collective_id=0, has_side_effects=True, vmem_limit_bytes=62 * 1024 * 1024
        ),
    )(out_grad, maps, inputs, gate_up, down)


def routing_maps(ids, gates, count):
    tok = ids.shape[0]
    chosen = ids[:, :, None] == jnp.arange(count, dtype=jnp.int32)
    named = jnp.any(chosen, axis=1)
    before = jnp.arange(tok)[:, None] > jnp.arange(tok)[None, :]
    slot = jnp.dot(
        before.astype(jnp.bfloat16), named.astype(jnp.bfloat16), preferred_element_type=jnp.float32
    )
    slot = jnp.where(named, slot, -1024.0)
    gate = jnp.sum(jnp.where(chosen, gates[:, :, None], 0.0), axis=1)
    return slot.T, gate.T


def per_device(out_grad, expert_ids, gates, expert_input, gate_up_weight, down_weight):
    inner, major, minor = lax.axis_size("i"), lax.axis_size("m"), lax.axis_size("n")
    plane = inner * minor
    tok = expert_ids.shape[0]
    sources, _, cps, width = expert_input.shape
    slot, gate = routing_maps(expert_ids, gates, sources)
    if (inner, major, minor, tok, cps % 8) == (4, 4, 2, 128, 0):
        maps = jnp.stack([slot, gate]).reshape(2, inner, major, minor, tok).transpose(2, 0, 1, 3, 4)
        token_grad, down_grad = fused(
            out_grad, maps.reshape(major, 2 * plane, tok),
            expert_input.reshape(inner, major, minor * cps, width), gate_up_weight[0], down_weight[0], cps,
        )
        return token_grad, down_grad[None]
    maps = jnp.stack([slot, gate]).reshape(2, inner, major, minor, tok).transpose(2, 0, 1, 3, 4)
    maps = lax.all_to_all(maps, "m", split_axis=0, concat_axis=0, tiled=True)
    slot, gate = maps[:, 0].reshape(major, plane, tok), maps[:, 1].reshape(major, plane, tok)
    blocks = lax.all_gather(out_grad, "m")
    pick = slot[:, :, None, :] == jnp.arange(cps, dtype=jnp.float32)[:, None]
    scale = jnp.sum(jnp.where(pick, gate[:, :, None, :], 0.0), axis=-1)
    pick = pick.astype(jnp.bfloat16)
    rows = jnp.einsum("mpct,mtd->pmcd", pick, blocks, preferred_element_type=jnp.float32)
    rows = (rows * scale.transpose(1, 0, 2)[..., None]).astype(jnp.bfloat16)
    rows = lax.all_to_all(rows, PLANE, split_axis=0, concat_axis=0, tiled=True)
    rows = rows.reshape(sources * cps, width)
    inputs = expert_input.reshape(inner, major, minor, cps, width).transpose(0, 2, 1, 3, 4)
    inputs = inputs.reshape(sources * cps, width)

    gate_up, down = gate_up_weight[0], down_weight[0]
    hidden_width = down.shape[0]
    pre = jnp.dot(inputs, gate_up, preferred_element_type=jnp.float32)
    act_a, act_b = pre[:, :hidden_width], pre[:, hidden_width:]
    sigma = jax.nn.sigmoid(act_a)
    silu_a = act_a * sigma
    hidden = (silu_a * act_b).astype(jnp.bfloat16)
    grad_h = lax.dot_general(
        rows, down, (((1,), (1,)), ((), ())), preferred_element_type=jnp.float32
    )
    grad_a = grad_h * act_b * sigma * (1.0 + act_a * (1.0 - sigma))
    grad_gu = jnp.concatenate([grad_a, grad_h * silu_a], axis=1).astype(jnp.bfloat16)
    slot_grad = lax.dot_general(
        grad_gu, gate_up, (((1,), (1,)), ((), ())), preferred_element_type=jnp.float32
    ).astype(jnp.bfloat16)
    down_grad = lax.dot_general(
        hidden, rows, (((0,), (0,)), ((), ())), preferred_element_type=jnp.float32
    ).astype(jnp.bfloat16)

    back = slot_grad.reshape(plane, major, cps, width)
    back = lax.all_to_all(back, PLANE, split_axis=0, concat_axis=0, tiled=True)
    part = jnp.einsum("mpct,pmcd->mtd", pick, back, preferred_element_type=jnp.float32)
    part = part.astype(jnp.bfloat16)
    part = lax.all_to_all(part, "m", split_axis=0, concat_axis=0, tiled=True)
    token_grad = jnp.sum(part.astype(jnp.float32), axis=0).astype(jnp.bfloat16)
    return token_grad, down_grad[None]


def solution(mesh):
    inner, outer = mesh.devices.shape
    major = 4
    fine = Mesh(mesh.devices.reshape(inner, major, outer // major), ("i", "m", "n"))
    every = ("i", "m", "n")
    placed = (
        P(every, None),
        P(every, None),
        P(every, None),
        P(None, every, None, None),
        P(every, None, None),
        P(every, None, None),
    )
    return jax.shard_map(
        per_device,
        mesh=fine,
        in_specs=placed,
        out_specs=(P(every, None), P(every, None, None)),
        check_vma=False,
    )
```

```python
import functools

import jax
import jax.numpy as jnp
from jax import lax
from jax.experimental import pallas as pl
from jax.experimental.pallas import tpu as pltpu
from jax.sharding import Mesh, PartitionSpec as P

PLANE = ("i", "n")
MESH = pl.DeviceIdType.MESH
F32, BF16 = jnp.float32, jnp.bfloat16
LANES = 512


def fused_kernel(
    cps, og_in, maps_in, x_in, wgu_in, wd_in, token_out, down_out,
    og, maps, pick, scale, send, rows, xs, back, pre, wgu, wd, dgu, hid, down, own, hold, part, got,
    load_sem, copy_sem, zs_sem, zr_sem, ms_sem, mr_sem, ds_sem, dr_sem, cs_sem, cr_sem, ps_sem, pr_sem,
):
    i, m, n = lax.axis_index("i"), lax.axis_index("m"), lax.axis_index("n")
    x, c = i // 2, i % 2
    zh, zl = m // 2, m % 2
    mine = i * 2 + n
    tok, width = og_in.shape
    hidden_width = wd_in.shape[0]
    pair = 2 * cps
    total = 8 * pair
    early = cps // 16 * 16
    late = pair - early
    early_at = pl.multiple_of(zl * late, 16)
    late_at = pl.multiple_of((1 - zl) * early, 16)

    def z_peer(j):
        return 2 * ((zh + j // 2) % 2) + (zl + j % 2) % 2

    def plane_peer(k):
        ki, kc, kn = k // 4, k // 2 % 2, k % 2
        return 2 * ((x + ki) % 2) + (c + kc) % 2, (n + kn) % 2

    def block_rows(which):
        return pl.ds(pl.multiple_of(which * tok, tok), tok)

    loads = [
        pltpu.make_async_copy(og_in, og.at[0, block_rows(zl)], load_sem.at[0]),
        pltpu.make_async_copy(maps_in.at[m], maps.at[0, zl], load_sem.at[1]),
        pltpu.make_async_copy(wgu_in, wgu, load_sem.at[2]),
    ]
    for g in range(2):
        for a in range(4):
            loads.append(
                pltpu.make_async_copy(
                    x_in.at[a, pl.ds(2 * ((zh + g) % 2), 2)],
                    xs.at[g, pl.ds(2 * a, 2)],
                    load_sem.at[3 + 4 * g + a],
                )
            )
    loads.append(pltpu.make_async_copy(wd_in, wd, load_sem.at[11]))
    for load in loads:
        load.start()

    barrier = pltpu.get_barrier_semaphore()
    for j in range(1, 4):
        pl.semaphore_signal(barrier, inc=1, device_id=(i, z_peer(j), n), device_id_type=MESH)
    for k in range(1, 8):
        pi, pn = plane_peer(k)
        pl.semaphore_signal(barrier, inc=1, device_id=(pi, m, pn), device_id_type=MESH)

    place = lax.broadcasted_iota(jnp.int32, (pair, tok), 0).astype(F32)

    def choose(g, which, first):
        for p in range(8):
            hit = place == maps[g, which, p : p + 1, :] + (cps * which).astype(F32)
            pick[g, p, :, block_rows(which)] = jnp.where(hit, 1.0, 0.0).astype(BF16)
            factor = jnp.sum(jnp.where(hit, maps[g, which, 8 + p : 9 + p, :], 0.0), axis=1, keepdims=True)
            factor = jnp.broadcast_to(factor, (pair, 128))
            scale[g, p] = factor if first else scale[g, p] + factor

    loads[1].wait()
    choose(0, zl, True)
    pl.semaphore_wait(barrier, 10)

    map_copies, block_copies = [], []
    for j in range(1, 4):
        there = z_peer(j)
        map_copies.append(
            pltpu.make_async_remote_copy(
                src_ref=maps_in.at[there], dst_ref=maps.at[j // 2, zl],
                send_sem=ms_sem.at[j], recv_sem=mr_sem.at[j],
                device_id=(i, there, n), device_id_type=MESH,
            )
        )
        block_copies.append(
            pltpu.make_async_remote_copy(
                src_ref=og.at[1, block_rows(zl)] if j == 3 else og_in, dst_ref=og.at[j // 2, block_rows(zl)],
                send_sem=zs_sem.at[j], recv_sem=zr_sem.at[j],
                device_id=(i, z_peer(j % 2 or 2), n), device_id_type=MESH,
            )
        )
    near_copy, cross_copy, forward_copy = block_copies
    for copy in map_copies:
        copy.start()
    near_copy.start()

    @pl.when(zh + zl == 1)
    def _():
        cross_copy.start()

    def lanes(t, size=LANES):
        return pl.ds(pl.multiple_of(t * size, size), size)

    order = (5, 7, 4, 1, 6, 3, 2)
    sent = []
    half = width // 2

    def dispatch(g, chunk, start, size, whole):
        tokens = slice(None) if whole else block_rows(zl)
        depth = 2 * tok if whole else tok
        weights = pick[g, :, pl.ds(start, size), tokens].reshape(8 * size, depth)
        factor = scale[g, :, pl.ds(start, size), :].reshape(8 * size, 128)[:, :1]

        def tile(t, _):
            out = jnp.dot(weights, og[g, tokens, lanes(t)], preferred_element_type=F32) * factor
            send[g, :, pl.ds(start, size), lanes(t)] = out.astype(BF16).reshape(8, size, LANES)
            return 0

        lax.fori_loop(0, width // LANES, tile, 0)
        copies = []
        for k in order:
            pi, pn = plane_peer(k)
            copy = pltpu.make_async_remote_copy(
                src_ref=send.at[g, pi * 2 + pn, pl.ds(start, size)],
                dst_ref=rows.at[g, mine, pl.ds(start, size)],
                send_sem=ds_sem.at[g, chunk, k], recv_sem=dr_sem.at[g, chunk, k],
                device_id=(pi, m, pn), device_id_type=MESH,
            )
            copy.start()
            copies.append(copy)
        here = pltpu.make_async_copy(
            send.at[g, mine, pl.ds(start, size)], rows.at[g, mine, pl.ds(start, size)], copy_sem.at[g, chunk]
        )
        here.start()
        sent.extend(copies)
        return copies, here

    def forward(g):
        for a in range(4):
            loads[3 + 4 * g + a].wait()

        def tile(t, _):
            out = jnp.dot(
                xs[g].reshape(total, width), wgu[:, lanes(t)], preferred_element_type=F32
            ).reshape(4, 4, cps, LANES)
            for a in range(2):
                for b in range(2):
                    pre[g, :, b * 2 + a, :, lanes(t)] = out[:, a * 2 + b]
            return 0

        lax.fori_loop(0, 2 * hidden_width // LANES, tile, 0)

    def backward(g, arriving, go):
        for copies, here in arriving:
            for copy in copies:
                copy.wait_recv()
            here.wait()
        if go:
            near_back.append(hand_back(0, 0))

        def first(t, _):
            size = 256
            at_b = pl.ds(pl.multiple_of(hidden_width + t * size, size), size)
            grad_h = lax.dot_general(
                rows[g].reshape(total, width), wd[lanes(t, size), :], (((1,), (1,)), ((), ())),
                preferred_element_type=F32,
            )
            act_a = pre[g, :, :, :, lanes(t, size)].reshape(total, size)
            act_b = pre[g, :, :, :, at_b].reshape(total, size)
            sigma = jax.nn.sigmoid(act_a)
            silu_a = act_a * sigma
            hid[g, :, lanes(t, size)] = (silu_a * act_b).astype(BF16)
            dgu[:, lanes(t, size)] = (
                grad_h * act_b * sigma * (1.0 + act_a * (1.0 - sigma))
            ).astype(BF16)
            dgu[:, at_b] = (grad_h * silu_a).astype(BF16)
            return 0

        lax.fori_loop(0, hidden_width // 256, first, 0)
        copies = []
        for h in range(2):
            def second(t, _):
                out = lax.dot_general(
                    dgu[...], wgu[lanes(t), :], (((1,), (1,)), ((), ())), preferred_element_type=F32
                )
                xs[g, :, :, lanes(t)] = out.astype(BF16).reshape(8, pair, LANES)
                return 0

            lax.fori_loop(h * half // LANES, (h + 1) * half // LANES, second, 0)
            if go:
                copies.append(hand_back(g, h))
        return copies

    def hand_back(g, h):
        cols = pl.ds(h * half, half)
        copies = []
        for k in order:
            pi, pn = plane_peer(k)
            copy = pltpu.make_async_remote_copy(
                src_ref=xs.at[g, pi * 2 + pn, :, cols], dst_ref=back.at[g, mine, :, cols],
                send_sem=cs_sem.at[g, h, k], recv_sem=cr_sem.at[g, h, k],
                device_id=(pi, m, pn), device_id_type=MESH,
            )
            copy.start()
            copies.append(copy)
        here = pltpu.make_async_copy(xs.at[g, mine, :, cols], back.at[g, mine, :, cols], copy_sem.at[g, 2 + h])
        here.start()
        sent.extend(copies)
        return copies, here

    def partial(g, which, h, put):
        weights = pick[g, :, :, block_rows(which)].reshape(total, tok)

        def tile(t, _):
            put(t, lax.dot_general(
                weights, back[g, :, :, lanes(t)].reshape(total, LANES), (((0,), (0,)), ((), ())),
                preferred_element_type=F32,
            ))
            return 0

        lax.fori_loop(h * half // LANES, (h + 1) * half // LANES, tile, 0)

    def keep(t, value):
        own[:, lanes(t)] = value

    def set_aside(t, value):
        hold[:, lanes(t)] = value

    def ship(j, h, to):
        cols = pl.ds(h * half, half)
        copy = pltpu.make_async_remote_copy(
            src_ref=part.at[j, :, cols], dst_ref=got.at[j, :, cols],
            send_sem=ps_sem.at[j, h], recv_sem=pr_sem.at[j, h],
            device_id=(i, z_peer(to), n), device_id_type=MESH,
        )
        copy.start()
        sent.append(copy)
        return copy

    def near_part(h, arriving):
        arrive(*arriving)

        def put(t, value):
            part[1, :, lanes(t)] = value.astype(BF16)

        partial(0, 1 - zl, h, put)
        copy = ship(1, h, 1)
        partial(0, zl, h, keep)
        return copy

    def far_part(h):
        def put(t, value):
            part[3, :, lanes(t)] = value.astype(BF16)

        partial(1, 1 - zl, h, put)
        copy = ship(3, h, 1)
        partial(1, zl, h, set_aside)
        copy.wait_recv()
        cols = pl.ds(h * half, half)
        part[2, :, cols] = (hold[:, cols] + got[3, :, cols].astype(F32)).astype(BF16)
        return ship(2, h, 2)

    def arrive(copies, here):
        for copy in copies:
            copy.wait_recv()
        here.wait()

    loads[0].wait()
    near = [dispatch(0, 0, early_at, early, False)]
    for copy in map_copies:
        copy.wait_recv()
    choose(0, 1 - zl, False)
    choose(1, zl, True)
    choose(1, 1 - zl, False)
    near_copy.wait_send()

    @pl.when(zh + zl != 1)
    def _():
        cross_copy.start()

    near_copy.wait_recv()
    near.append(dispatch(0, 1, late_at, late, True))
    loads[2].wait()
    forward(0)
    cross_copy.wait_recv()
    forward_copy.start()
    far = [dispatch(1, 0, early_at, early, False)]
    forward(1)
    loads[11].wait()
    forward_copy.wait_recv()
    far.append(dispatch(1, 1, late_at, late, True))
    backward(0, near, False)
    near_back = []
    far_back = backward(1, far, True)
    def gradient(t, _):
        out = lax.dot_general(
            hid[...].reshape(2 * total, hidden_width), rows[:, :, :, lanes(t)].reshape(2 * total, LANES),
            (((0,), (0,)), ((), ())), preferred_element_type=F32,
        )
        down[:, lanes(t)] = out.astype(BF16)
        return 0

    lax.fori_loop(0, width // LANES, gradient, 0)
    result = pltpu.make_async_copy(down, down_out, load_sem.at[12])
    result.start()
    ends = [near_part(0, near_back[0])]
    arrive(*far_back[0])
    near_back.append(hand_back(0, 1))
    ends.append(far_part(0))
    arrive(*far_back[1])
    ends.append(far_part(1))
    ends.append(near_part(1, near_back[1]))
    for copy in ends:
        copy.wait_recv()
    token_out[...] = (
        own[...] + got[1].astype(F32) + got[2].astype(F32)
    ).astype(BF16)
    result.wait()
    for copy in map_copies + [cross_copy, forward_copy] + sent:
        copy.wait_send()


def fused(out_grad, maps, inputs, gate_up, down, cps):
    tok, width = out_grad.shape
    hidden_width = down.shape[0]
    pair = 2 * cps
    anywhere = pl.BlockSpec(memory_space=pl.ANY)
    local = pl.BlockSpec(memory_space=pltpu.VMEM)
    dma = pltpu.SemaphoreType.DMA
    return pl.pallas_call(
        functools.partial(fused_kernel, cps),
        out_shape=(
            jax.ShapeDtypeStruct((tok, width), BF16),
            jax.ShapeDtypeStruct((hidden_width, width), BF16),
        ),
        in_specs=[anywhere] * 5,
        out_specs=(local, anywhere),
        scratch_shapes=[
            pltpu.VMEM((2, 2 * tok, width), BF16),
            pltpu.VMEM((2, 2, 16, tok), F32),
            pltpu.VMEM((2, 8, pair, 2 * tok), BF16),
            pltpu.VMEM((2, 8, pair, 128), F32),
            pltpu.VMEM((2, 8, pair, width), BF16),
            pltpu.VMEM((2, 8, pair, width), BF16),
            pltpu.VMEM((2, 8, pair, width), BF16),
            pltpu.VMEM((2, 8, pair, width), BF16),
            pltpu.VMEM((2, 4, 4, cps, 2 * hidden_width), F32),
            pltpu.VMEM((width, 2 * hidden_width), BF16),
            pltpu.VMEM((hidden_width, width), BF16),
            pltpu.VMEM((8 * pair, 2 * hidden_width), BF16),
            pltpu.VMEM((2, 8 * pair, hidden_width), BF16),
            pltpu.VMEM((hidden_width, width), BF16),
            pltpu.VMEM((tok, width), F32),
            pltpu.VMEM((tok, width), F32),
            pltpu.VMEM((4, tok, width), BF16),
            pltpu.VMEM((4, tok, width), BF16),
            dma((13,)), dma((2, 4)), dma((4,)), dma((4,)), dma((4,)), dma((4,)),
            dma((2, 2, 8)), dma((2, 2, 8)), dma((2, 2, 8)), dma((2, 2, 8)), dma((4, 2)), dma((4, 2)),
        ],
        compiler_params=pltpu.CompilerParams(
            collective_id=0, has_side_effects=True, vmem_limit_bytes=62 * 1024 * 1024
        ),
    )(out_grad, maps, inputs, gate_up, down)


def routing_maps(ids, gates, count):
    tok = ids.shape[0]
    chosen = ids[:, :, None] == jnp.arange(count, dtype=jnp.int32)
    named = jnp.any(chosen, axis=1)
    before = jnp.arange(tok)[:, None] > jnp.arange(tok)[None, :]
    slot = jnp.dot(
        before.astype(jnp.bfloat16), named.astype(jnp.bfloat16), preferred_element_type=jnp.float32
    )
    slot = jnp.where(named, slot, -1024.0)
    gate = jnp.sum(jnp.where(chosen, gates[:, :, None], 0.0), axis=1)
    return slot.T, gate.T


def per_device(out_grad, expert_ids, gates, expert_input, gate_up_weight, down_weight):
    inner, major, minor = lax.axis_size("i"), lax.axis_size("m"), lax.axis_size("n")
    plane = inner * minor
    tok = expert_ids.shape[0]
    sources, _, cps, width = expert_input.shape
    slot, gate = routing_maps(expert_ids, gates, sources)
    if (inner, major, minor, tok, cps % 8) == (4, 4, 2, 128, 0):
        maps = jnp.stack([slot, gate]).reshape(2, inner, major, minor, tok).transpose(2, 0, 1, 3, 4)
        token_grad, down_grad = fused(
            out_grad, maps.reshape(major, 2 * plane, tok),
            expert_input.reshape(inner, major, minor * cps, width), gate_up_weight[0], down_weight[0], cps,
        )
        return token_grad, down_grad[None]
    maps = jnp.stack([slot, gate]).reshape(2, inner, major, minor, tok).transpose(2, 0, 1, 3, 4)
    maps = lax.all_to_all(maps, "m", split_axis=0, concat_axis=0, tiled=True)
    slot, gate = maps[:, 0].reshape(major, plane, tok), maps[:, 1].reshape(major, plane, tok)
    blocks = lax.all_gather(out_grad, "m")
    pick = slot[:, :, None, :] == jnp.arange(cps, dtype=jnp.float32)[:, None]
    scale = jnp.sum(jnp.where(pick, gate[:, :, None, :], 0.0), axis=-1)
    pick = pick.astype(jnp.bfloat16)
    rows = jnp.einsum("mpct,mtd->pmcd", pick, blocks, preferred_element_type=jnp.float32)
    rows = (rows * scale.transpose(1, 0, 2)[..., None]).astype(jnp.bfloat16)
    rows = lax.all_to_all(rows, PLANE, split_axis=0, concat_axis=0, tiled=True)
    rows = rows.reshape(sources * cps, width)
    inputs = expert_input.reshape(inner, major, minor, cps, width).transpose(0, 2, 1, 3, 4)
    inputs = inputs.reshape(sources * cps, width)

    gate_up, down = gate_up_weight[0], down_weight[0]
    hidden_width = down.shape[0]
    pre = jnp.dot(inputs, gate_up, preferred_element_type=jnp.float32)
    act_a, act_b = pre[:, :hidden_width], pre[:, hidden_width:]
    sigma = jax.nn.sigmoid(act_a)
    silu_a = act_a * sigma
    hidden = (silu_a * act_b).astype(jnp.bfloat16)
    grad_h = lax.dot_general(
        rows, down, (((1,), (1,)), ((), ())), preferred_element_type=jnp.float32
    )
    grad_a = grad_h * act_b * sigma * (1.0 + act_a * (1.0 - sigma))
    grad_gu = jnp.concatenate([grad_a, grad_h * silu_a], axis=1).astype(jnp.bfloat16)
    slot_grad = lax.dot_general(
        grad_gu, gate_up, (((1,), (1,)), ((), ())), preferred_element_type=jnp.float32
    ).astype(jnp.bfloat16)
    down_grad = lax.dot_general(
        hidden, rows, (((0,), (0,)), ((), ())), preferred_element_type=jnp.float32
    ).astype(jnp.bfloat16)

    back = slot_grad.reshape(plane, major, cps, width)
    back = lax.all_to_all(back, PLANE, split_axis=0, concat_axis=0, tiled=True)
    part = jnp.einsum("mpct,pmcd->mtd", pick, back, preferred_element_type=jnp.float32)
    part = part.astype(jnp.bfloat16)
    part = lax.all_to_all(part, "m", split_axis=0, concat_axis=0, tiled=True)
    token_grad = jnp.sum(part.astype(jnp.float32), axis=0).astype(jnp.bfloat16)
    return token_grad, down_grad[None]


def solution(mesh):
    inner, outer = mesh.devices.shape
    major = 4
    fine = Mesh(mesh.devices.reshape(inner, major, outer // major), ("i", "m", "n"))
    every = ("i", "m", "n")
    placed = (
        P(every, None),
        P(every, None),
        P(every, None),
        P(None, every, None, None),
        P(every, None, None),
        P(every, None, None),
    )
    return jax.shard_map(
        per_device,
        mesh=fine,
        in_specs=placed,
        out_specs=(P(every, None), P(every, None, None)),
        check_vma=False,
    )
```
